32 devices in a mesh: grp: 2 (over x), row: 16 (over z, y, core).
Axes of the slice: x: 2, y: 2, z: 4, core: 2. Of those that a mesh axis runs over, the one named last changes fastest.
Arguments:
- slot_pairs: int32 [16512, 2], P(('grp', 'row')), parts along dimension 0, may hold values from -1 to 127, as said below
- lag_table: int32 [256, 128], P('grp'), parts along dimension 0, may hold values from 0 to 3, as said below
- kernel: float32 [16512, 128, 128], P(('grp', 'row')), parts along dimension 0, may hold values from -0.046875 to 0.046875
- history: float32 [8, 32, 16384], P('grp', None, 'row'), parts along dimension 0, may hold values from -6 to 6
Outputs:
- field: float32 [64, 16384], P('grp', 'row'), parts along dimension 0
The draws below stay inside these ranges and needn't reach their ends.
There are 2 independent parts, one for each index of `grp`. The reference program is written for one: setup_inputs(seed, part) draws one part's arguments, and reference() takes and returns one part's arrays. A program takes and returns all parts, laid end to end along the dimension named above; each array names one. Nothing has to cross between parts.
Inputs may be any that keep to these rules, and one draw needn't show every extreme that they name: `slot_pairs`: each pair (i, j) with i <= j < 128 stands in exactly one slot, in an order drawn from the seed; every other slot holds -1 in both columns. `lag_table`: symmetric.
All inputs are finite; a program needn't handle non-finite values.
Results may differ from the reference program's by a relative error of at most 0.0003.
Values sent between devices are 32-bit elements; how exact they have to be, the bound alone decides.
A program may use at most 128 MiB of HBM per device.

```python
import jax
import jax.numpy as jnp
from jax import lax

N = 16384
EXC = 32
LAGS = 4
BLOCK = 128
NB = 128
NPAIR = 8256
SLOTS = 8256


def draw_slot_pairs(key, part):
    key = jax.random.fold_in(key, 11)
    order = jax.random.permutation(key, SLOTS).astype(jnp.int32)
    block_rows = jnp.arange(NB, dtype=jnp.int32)
    starts = block_rows * NB - block_rows * (block_rows - 1) // 2
    row_ids = jnp.sum((order[:, None] >= starts[None, :]).astype(jnp.int32), axis=1) - 1
    col_ids = row_ids + order - starts[row_ids]
    live = order < NPAIR
    row_ids = jnp.where(live, row_ids, -1)
    col_ids = jnp.where(live, col_ids, -1)
    return jnp.stack([row_ids, col_ids], axis=1).astype(jnp.int32)


def draw_lag_table(key, part):
    key = jax.random.fold_in(key, 23)
    base = jax.random.randint(key, (NB, NB), 0, LAGS)
    upper = jnp.arange(NB)[:, None] <= jnp.arange(NB)[None, :]
    return jnp.where(upper, base, base.T).astype(jnp.int32)


def block_scale(stream_key, dims, cuts, smallest, top_value):
    level = 1.0
    for position, shards_of in cuts:
        steps = jax.random.uniform(jax.random.fold_in(jax.random.fold_in(stream_key, 6), position), (shards_of,), jnp.float32, smallest / len(cuts), top_value / len(cuts))
        level = level * jnp.repeat(jnp.exp(steps), dims[position] // shards_of).reshape((-1,) + (1,) * (len(dims) - 1 - position))
    return level


def bell_draw(stream_key, dims, deviation, reach, cuts=(), held_as=jnp.bfloat16):
    values = jax.random.normal(stream_key, dims, jnp.float32) * deviation
    if len(cuts) > 0:
        values = block_scale(stream_key, dims, cuts, -0.22, 0.18) * values
    return jnp.clip(values, min=-reach, max=reach).astype(held_as)


def setup_inputs(seed: int = 0, part: int = 0) -> dict:
    seeds = jax.random.split(jax.random.key(seed), 5)
    own_keys = jax.random.split(jax.random.fold_in(seeds[4], part), 5)
    slot_pairs = draw_slot_pairs(jax.random.fold_in(jax.random.fold_in(seeds[4], part), 71), part)
    lag_table = draw_lag_table(jax.random.fold_in(jax.random.fold_in(seeds[4], part), 71), part)
    kernel = bell_draw(own_keys[2], (SLOTS, BLOCK, BLOCK), N ** -0.5, 0.046875, ((0, 16),), jnp.float32)
    history = bell_draw(own_keys[3], (LAGS, EXC, N), 1.0, 6.0, ((2, 16),), jnp.float32)
    return {"slot_pairs": slot_pairs, "lag_table": lag_table, "kernel": kernel, "history": history}


def reference(slot_pairs, lag_table, kernel, history):
    n_blocks = N // BLOCK
    panels = history.reshape(LAGS, EXC, n_blocks, BLOCK)
    row_ids = jnp.maximum(slot_pairs[:, 0], 0).astype(jnp.int32)
    col_ids = jnp.maximum(slot_pairs[:, 1], 0).astype(jnp.int32)
    live_mask = (slot_pairs[:, 0] >= 0).astype(jnp.float32)
    lag_ids = lag_table[row_ids, col_ids]

    def step(total, item):
        block, row_id, col_id, lag_id, live = item
        far_panel = panels[lag_id, :, col_id, :]
        near_panel = panels[lag_id, :, row_id, :]
        direct = jnp.dot(far_panel, block.T, precision=lax.Precision.HIGHEST, preferred_element_type=jnp.float32) * live
        off_diag = live * (row_id != col_id).astype(jnp.float32)
        mirror = jnp.dot(near_panel, block, precision=lax.Precision.HIGHEST, preferred_element_type=jnp.float32) * off_diag
        total = total.at[:, row_id, :].add(direct)
        total = total.at[:, col_id, :].add(mirror)
        return total, None

    start = jnp.zeros((EXC, n_blocks, BLOCK), jnp.float32)
    total, unused = lax.scan(step, start, (kernel, row_ids, col_ids, lag_ids, live_mask))
    return total.reshape(EXC, N)
```

```python
import functools

import jax
import jax.numpy as jnp
from jax import lax
from jax.experimental import pallas as pl
from jax.experimental.pallas import tpu as pltpu
from jax.sharding import PartitionSpec as P

MESH = pl.DeviceIdType.MESH
MIB = 1024 * 1024


def grid_of(rows):
    chips = rows // 2
    side_b = 1
    while side_b * side_b * 4 <= chips:
        side_b *= 2
    return chips // side_b, side_b


def place(side_b):
    r = lax.axis_index("row")
    core = lax.rem(r, 2)
    chip = r // 2
    return r, chip // side_b, lax.rem(chip, side_b), core


def greet(side_a, side_b, a, b, core):
    barrier = pltpu.get_barrier_semaphore()

    def signal(row):
        pl.semaphore_signal(barrier, inc=1, device_id={"row": row}, device_id_type=MESH)

    for d in range(1, side_a):
        signal((lax.rem(a + d, side_a) * side_b + b) * 2 + core)
    for d in range(1, side_b):
        signal((a * side_b + lax.rem(b + d, side_b)) * 2 + core)
    signal((a * side_b + b) * 2 + 1 - core)
    pl.semaphore_wait(barrier, side_a + side_b - 1)


def gather_kernel(side_a, side_b, group, h_ref, g_ref, own, local_sem, z_sem, y_sem, c_sem, recv_sem):
    r, a, b, core = place(side_b)
    lags = h_ref.shape[0]
    width = g_ref.shape[3]
    per = h_ref.shape[2] // width
    parts = lags // group
    greet(side_a, side_b, a, b, core)
    for k in range(lags):
        for m in range(per):
            own[k, m] = h_ref[k, :, m * width : (m + 1) * width]

    def row_of(a_, b_, c_):
        return (a_ * side_b + b_) * 2 + c_

    def chunk(k, row):
        return g_ref.at[pl.ds(k * group, group), pl.ds(row * per, per)]

    def copy(k, origin, target, send, mine=False):
        src = own.at[pl.ds(k * group, group)] if mine else chunk(k, origin)
        return pltpu.make_async_remote_copy(
            src_ref=src,
            dst_ref=chunk(k, origin),
            send_sem=send,
            recv_sem=recv_sem.at[k, origin],
            device_id={"row": target},
            device_id_type=MESH,
        )

    sent = []

    def send(*args, **kw):
        c = copy(*args, **kw)
        c.start()
        sent.append(c)

    def arrived(k, origin):
        copy(k, origin, row_of(a, b, 1 - core), c_sem.at[k, 0]).wait_recv()

    local = []
    for k in range(parts):
        for d in range(1, side_a):
            send(k, r, row_of(lax.rem(a + d, side_a), b, core), z_sem.at[k, d], mine=True)
        for e in range(1, side_b):
            send(k, r, row_of(a, lax.rem(b + e, side_b), core), y_sem.at[k, 0, e], mine=True)
        send(k, r, row_of(a, b, 1 - core), c_sem.at[k, 0], mine=True)
        c = pltpu.make_async_copy(own.at[pl.ds(k * group, group)], chunk(k, r), local_sem.at[k])
        c.start()
        local.append(c)

    def column(k):
        for d in range(1, side_a):
            origin = row_of(lax.rem(a + d, side_a), b, core)
            arrived(k, origin)
            for e in range(1, side_b):
                send(k, origin, row_of(a, lax.rem(b + e, side_b), core), y_sem.at[k, d, e])
            send(k, origin, row_of(a, b, 1 - core), c_sem.at[k, d])

    def across(k):
        for d in range(side_a):
            for e in range(1, side_b):
                origin = row_of(lax.rem(a + d, side_a), lax.rem(b + e, side_b), core)
                arrived(k, origin)
                send(k, origin, row_of(a, b, 1 - core), c_sem.at[k, e * side_a + d])

    for k in range(parts):
        column(k)
        if k > 0:
            across(k - 1)
    across(parts - 1)
    for k in range(parts):
        for d in range(side_a):
            for e in range(side_b):
                arrived(k, row_of(lax.rem(a + d, side_a), lax.rem(b + e, side_b), 1 - core))
    for c in local:
        c.wait()
    for c in sent:
        c.wait_send()


def gather_history(history, rows, width):
    lags, exc, local = history.shape
    per = local // width
    side_a, side_b = grid_of(rows)
    group = 1 if rows <= 16 else lags
    parts = lags // group
    return pl.pallas_call(
        functools.partial(gather_kernel, side_a, side_b, group),
        out_shape=jax.ShapeDtypeStruct((lags, rows * per, exc, width), jnp.float32),
        in_specs=[pl.BlockSpec(memory_space=pltpu.VMEM)],
        out_specs=pl.BlockSpec(memory_space=pl.ANY),
        scratch_shapes=[
            pltpu.VMEM((lags, per, exc, width), jnp.float32),
            pltpu.SemaphoreType.DMA((parts,)),
            pltpu.SemaphoreType.DMA((parts, side_a)),
            pltpu.SemaphoreType.DMA((parts, side_a, side_b)),
            pltpu.SemaphoreType.DMA((parts, side_a * side_b)),
            pltpu.SemaphoreType.DMA((parts, rows)),
        ],
        compiler_params=pltpu.CompilerParams(collective_id=0, has_side_effects=True),
        name="gather_history",
    )(history)


def split(x):
    hi = x.astype(jnp.bfloat16)
    lo = (x - hi.astype(jnp.float32)).astype(jnp.bfloat16)
    return hi, lo


def product_kernel(slots, pairs, lag, g_ref, k_ref, t_ref):
    step = pl.program_id(0)
    exc = g_ref.shape[2]
    blocks = g_ref.shape[1]

    @pl.when(step == 0)
    def _():
        t_ref[...] = jnp.zeros_like(t_ref)

    def panel(k, col):
        hi, lo = split(g_ref[k, col])
        return jnp.concatenate(
            [jnp.concatenate([hi, hi], axis=1), jnp.concatenate([lo, lo], axis=1)], axis=0
        )

    for q in range(slots):
        s = step * slots + q
        i = pairs[2 * s]
        j = pairs[2 * s + 1]
        live = i >= 0
        row = jnp.maximum(i, 0)
        col = jnp.maximum(j, 0)
        k = lag[row, col]
        hi, lo = split(k_ref[q])
        far = lax.dot_general(
            panel(k, col),
            jnp.concatenate([hi, lo], axis=1),
            (((1,), (1,)), ((), ())),
            preferred_element_type=jnp.float32,
        )
        near = lax.dot_general(
            panel(k, row),
            jnp.concatenate([hi, lo], axis=0),
            (((1,), (0,)), ((), ())),
            preferred_element_type=jnp.float32,
        )
        to_row = jnp.where(live, i, blocks)
        to_col = jnp.where(jnp.logical_and(live, i != j), j, blocks)
        t_ref[to_row] += far[:exc] + far[exc:]
        t_ref[to_col] += near[:exc] + near[exc:]


def products(slot_pairs, lag_table, kernel, panels):
    n = kernel.shape[0]
    width = kernel.shape[1]
    lags, blocks, exc, _ = panels.shape
    slots = max(d for d in range(1, 13) if n % d == 0)
    return pl.pallas_call(
        functools.partial(product_kernel, slots),
        out_shape=jax.ShapeDtypeStruct((blocks + 1, exc, width), jnp.float32),
        grid_spec=pltpu.PrefetchScalarGridSpec(
            num_scalar_prefetch=2,
            grid=(n // slots,),
            in_specs=[
                pl.BlockSpec(panels.shape, lambda s, *_: (0, 0, 0, 0), pipeline_mode=pl.Buffered(1)),
                pl.BlockSpec((slots, width, width), lambda s, *_: (s, 0, 0)),
            ],
            out_specs=pl.BlockSpec((blocks + 1, exc, width), lambda s, *_: (0, 0, 0)),
        ),
        compiler_params=pltpu.CompilerParams(
            dimension_semantics=("arbitrary",), vmem_limit_bytes=40 * MIB
        ),
        cost_estimate=pl.CostEstimate(
            flops=n * width * width * exc * 16,
            bytes_accessed=n * width * width * 4 + panels.size * 4,
            transcendentals=0,
        ),
        name="block_products",
    )(slot_pairs.reshape(-1), lag_table, panels, kernel)


def scatter_kernel(side_a, side_b, per, t_ref, o_ref, buf1, buf2, buf3, sum2, sum3, s1, r1, s2, r2, s3, r3):
    r, a, b, core = place(side_b)
    width = t_ref.shape[2]
    greet(side_a, side_b, a, b, core)

    def row_of(a_, b_, c_):
        return (a_ * side_b + b_) * 2 + c_

    def part(row):
        return pl.ds(row * per, per)

    def remote(src, dst, ssem, rsem, target):
        return pltpu.make_async_remote_copy(
            src_ref=src, dst_ref=dst, send_sem=ssem, recv_sem=rsem,
            device_id={"row": target}, device_id_type=MESH,
        )

    sent = []
    order = [(d, e) for e in range(side_b - 1, -1, -1) for d in list(range(1, side_a)) + [0]]

    def at(d, e):
        return lax.rem(a + d, side_a), lax.rem(b + e, side_b)

    peer = row_of(a, b, 1 - core)

    def to_core(d, e):
        a_, b_ = at(d, e)
        chip = a_ * side_b + b_
        return remote(
            t_ref.at[part(row_of(a_, b_, 1 - core))], buf1.at[chip], s1.at[chip], r1.at[chip], peer
        )

    for d, e in order:
        c = to_core(d, e)
        c.start()
        sent.append(c)

    def core_sum(d, e):
        a_, b_ = at(d, e)
        to_core(d, e).wait_recv()
        return t_ref[part(row_of(a_, b_, core))] + buf1[a_ * side_b + b_]

    for d, e in order:
        a_, b_ = at(d, e)
        if e > 0:
            sum2[e - 1, d] = core_sum(d, e)
            c = remote(sum2.at[e - 1, d], buf2.at[b, a_], s2.at[e - 1, d], r2.at[b, a_], row_of(a, b_, core))
            c.start()
            sent.append(c)
            continue
        total = core_sum(d, 0)
        for e2 in range(1, side_b):
            from_b = lax.rem(b + e2, side_b)
            remote(
                sum2.at[e2 - 1, d], buf2.at[from_b, a_], s2.at[e2 - 1, d], r2.at[from_b, a_], row_of(a, from_b, core)
            ).wait_recv()
            total = total + buf2[from_b, a_]
        if d > 0:
            sum3[d] = total
            c = remote(sum3.at[d], buf3.at[a], s3.at[d], r3.at[a], row_of(a_, b, core))
            c.start()
            sent.append(c)
            continue
        sum3[0] = total
    for d in range(1, side_a):
        from_a = lax.rem(a + d, side_a)
        remote(sum3.at[d], buf3.at[from_a], s3.at[d], r3.at[from_a], row_of(from_a, b, core)).wait_recv()
    for m in range(per):
        total = sum3[0, m]
        for d in range(1, side_a):
            total = total + buf3[lax.rem(a + d, side_a), m]
        o_ref[:, m * width : (m + 1) * width] = total
    for c in sent:
        c.wait_send()


def scatter_sum(totals, rows, blocks):
    _, exc, width = totals.shape
    per = blocks // rows
    side_a, side_b = grid_of(rows)
    chips = side_a * side_b
    dma = pltpu.SemaphoreType.DMA
    return pl.pallas_call(
        functools.partial(scatter_kernel, side_a, side_b, per),
        out_shape=jax.ShapeDtypeStruct((exc, per * width), jnp.float32),
        in_specs=[pl.BlockSpec(memory_space=pltpu.VMEM)],
        out_specs=pl.BlockSpec(memory_space=pltpu.VMEM),
        scratch_shapes=[
            pltpu.VMEM((chips, per, exc, width), jnp.float32),
            pltpu.VMEM((side_b, side_a, per, exc, width), jnp.float32),
            pltpu.VMEM((side_a, per, exc, width), jnp.float32),
            pltpu.VMEM((max(side_b - 1, 1), side_a, per, exc, width), jnp.float32),
            pltpu.VMEM((side_a, per, exc, width), jnp.float32),
            dma((chips,)),
            dma((chips,)),
            dma((max(side_b - 1, 1), side_a)),
            dma((side_b, side_a)),
            dma((side_a,)),
            dma((side_a,)),
        ],
        compiler_params=pltpu.CompilerParams(
            collective_id=1, has_side_effects=True, vmem_limit_bytes=24 * MIB
        ),
        name="scatter_sum",
    )(totals)


def body(rows, slot_pairs, lag_table, kernel, history):
    width = kernel.shape[1]
    panels = gather_history(history, rows, width)
    totals = products(slot_pairs, lag_table, kernel, panels)
    return scatter_sum(totals, rows, panels.shape[1])


def solution(mesh):
    return jax.shard_map(
        functools.partial(body, mesh.shape["row"]),
        mesh=mesh,
        in_specs=(
            P(("grp", "row"), None),
            P("grp", None),
            P(("grp", "row"), None, None),
            P("grp", None, "row"),
        ),
        out_specs=P("grp", "row"),
        check_vma=False,
    )
```

```python
import functools

import jax
import jax.numpy as jnp
from jax import lax
from jax.experimental import pallas as pl
from jax.experimental.pallas import tpu as pltpu
from jax.sharding import PartitionSpec as P

MESH = pl.DeviceIdType.MESH
MIB = 1024 * 1024


def grid_of(rows):
    chips = rows // 2
    side_b = 1
    while side_b * side_b * 4 <= chips:
        side_b *= 2
    return chips // side_b, side_b


def place(side_b):
    r = lax.axis_index("row")
    core = lax.rem(r, 2)
    chip = r // 2
    return r, chip // side_b, lax.rem(chip, side_b), core


def greet(side_a, side_b, a, b, core):
    barrier = pltpu.get_barrier_semaphore()

    def signal(row):
        pl.semaphore_signal(barrier, inc=1, device_id={"row": row}, device_id_type=MESH)

    for d in range(1, side_a):
        signal((lax.rem(a + d, side_a) * side_b + b) * 2 + core)
    for d in range(1, side_b):
        signal((a * side_b + lax.rem(b + d, side_b)) * 2 + core)
    signal((a * side_b + b) * 2 + 1 - core)
    pl.semaphore_wait(barrier, side_a + side_b - 1)


def gather_kernel(side_a, side_b, group, h_ref, g_ref, own, local_sem, z_sem, y_sem, c_sem, recv_sem):
    r, a, b, core = place(side_b)
    lags = h_ref.shape[0]
    width = g_ref.shape[3]
    per = h_ref.shape[2] // width
    parts = lags // group
    greet(side_a, side_b, a, b, core)
    for k in range(lags):
        for m in range(per):
            own[k, m] = h_ref[k, :, m * width : (m + 1) * width]

    def row_of(a_, b_, c_):
        return (a_ * side_b + b_) * 2 + c_

    def chunk(k, row):
        return g_ref.at[pl.ds(k * group, group), pl.ds(row * per, per)]

    def copy(k, origin, target, send, mine=False):
        src = own.at[pl.ds(k * group, group)] if mine else chunk(k, origin)
        return pltpu.make_async_remote_copy(
            src_ref=src,
            dst_ref=chunk(k, origin),
            send_sem=send,
            recv_sem=recv_sem.at[k, origin],
            device_id={"row": target},
            device_id_type=MESH,
        )

    def arrived(k, origin):
        copy(k, origin, row_of(a, b, 1 - core), c_sem.at[k, 0]).wait_recv()

    def inside(a_):
        return jnp.logical_and(a_ >= 0, a_ < side_a)

    hops = [(1, 0)] + [(sign, d) for d in range(1, side_a) for sign in (1, -1)]

    def along(k, sign, d, act):
        @pl.when(inside(a + sign))
        def _():
            act(copy(k, row_of(a - sign * d, b, core), row_of(a + sign, b, core), z_sem.at[k, (sign + 1) // 2, d], d == 0))

    def beside(k, sign, d, act):
        origin = row_of(a - sign * d, b, core)
        for e in range(1, side_b):
            act(copy(k, origin, row_of(a, lax.rem(b + e, side_b), core), y_sem.at[k, a - sign * d, e], d == 0))

    def to_core(k, origin, act, mine=False):
        act(copy(k, origin, row_of(a, b, 1 - core), c_sem.at[k, origin // 2], mine))

    def start(c):
        c.start()

    def finish(c):
        c.wait_send()

    local = []
    for k in range(parts):
        along(k, 1, 0, start)
        along(k, -1, 0, start)
        beside(k, 1, 0, start)
        to_core(k, r, start, True)
        c = pltpu.make_async_copy(own.at[pl.ds(k * group, group)], chunk(k, r), local_sem.at[k])
        c.start()
        local.append(c)

    def column(k):
        for sign, d in hops[1:]:

            @pl.when(inside(a - sign * d))
            def _():
                origin = row_of(a - sign * d, b, core)
                arrived(k, origin)
                along(k, sign, d, start)
                beside(k, sign, d, start)
                to_core(k, origin, start)

    def across(k):
        for sign, d in hops:

            @pl.when(inside(a - sign * d))
            def _():
                for e in range(1, side_b):
                    origin = row_of(a - sign * d, lax.rem(b + e, side_b), core)
                    arrived(k, origin)
                    to_core(k, origin, start)

    for k in range(parts):
        column(k)
        if k > 0:
            across(k - 1)
    across(parts - 1)
    for k in range(parts):
        along(k, 1, 0, finish)
        along(k, -1, 0, finish)
        beside(k, 1, 0, finish)
        for sign, d in hops[1:]:

            @pl.when(inside(a - sign * d))
            def _():
                along(k, sign, d, finish)
                beside(k, sign, d, finish)

        for a_ in range(side_a):
            for b_ in range(side_b):
                arrived(k, row_of(a_, b_, 1 - core))
                to_core(k, row_of(a_, b_, core), finish)
    for c in local:
        c.wait()


def gather_history(history, rows, width):
    lags, exc, local = history.shape
    per = local // width
    side_a, side_b = grid_of(rows)
    group = 1 if rows <= 16 else lags
    parts = lags // group
    return pl.pallas_call(
        functools.partial(gather_kernel, side_a, side_b, group),
        out_shape=jax.ShapeDtypeStruct((lags, rows * per, exc, width), jnp.float32),
        in_specs=[pl.BlockSpec(memory_space=pltpu.VMEM)],
        out_specs=pl.BlockSpec(memory_space=pltpu.VMEM),
        scratch_shapes=[
            pltpu.VMEM((lags, per, exc, width), jnp.float32),
            pltpu.SemaphoreType.DMA((parts,)),
            pltpu.SemaphoreType.DMA((parts, 2, side_a)),
            pltpu.SemaphoreType.DMA((parts, side_a, side_b)),
            pltpu.SemaphoreType.DMA((parts, side_a * side_b)),
            pltpu.SemaphoreType.DMA((parts, rows)),
        ],
        compiler_params=pltpu.CompilerParams(collective_id=0, has_side_effects=True, vmem_limit_bytes=24 * MIB),
        name="gather_history",
    )(history)


def split(x):
    hi = x.astype(jnp.bfloat16)
    lo = (x - hi.astype(jnp.float32)).astype(jnp.bfloat16)
    return hi, lo


def product_kernel(slots, pairs, lag, g_ref, k_ref, t_ref):
    step = pl.program_id(0)
    exc = g_ref.shape[2]
    blocks = g_ref.shape[1]

    @pl.when(step == 0)
    def _():
        t_ref[...] = jnp.zeros_like(t_ref)

    def panel(k, col):
        hi, lo = split(g_ref[k, col])
        return jnp.concatenate(
            [jnp.concatenate([hi, hi], axis=1), jnp.concatenate([lo, lo], axis=1)], axis=0
        )

    for q in range(slots):
        s = step * slots + q
        i = pairs[2 * s]
        j = pairs[2 * s + 1]
        live = i >= 0
        row = jnp.maximum(i, 0)
        col = jnp.maximum(j, 0)
        k = lag[row, col]
        hi, lo = split(k_ref[q])
        far = lax.dot_general(
            panel(k, col),
            jnp.concatenate([hi, lo], axis=1),
            (((1,), (1,)), ((), ())),
            preferred_element_type=jnp.float32,
        )
        near = lax.dot_general(
            panel(k, row),
            jnp.concatenate([hi, lo], axis=0),
            (((1,), (0,)), ((), ())),
            preferred_element_type=jnp.float32,
        )
        to_row = jnp.where(live, i, blocks)
        to_col = jnp.where(jnp.logical_and(live, i != j), j, blocks)
        t_ref[to_row] += far[:exc] + far[exc:]
        t_ref[to_col] += near[:exc] + near[exc:]


def products(slot_pairs, lag_table, kernel, panels):
    n = kernel.shape[0]
    width = kernel.shape[1]
    lags, blocks, exc, _ = panels.shape
    slots = max(d for d in range(1, 87) if n % d == 0)
    return pl.pallas_call(
        functools.partial(product_kernel, slots),
        out_shape=jax.ShapeDtypeStruct((blocks + 1, exc, width), jnp.float32),
        grid_spec=pltpu.PrefetchScalarGridSpec(
            num_scalar_prefetch=2,
            grid=(n // slots,),
            in_specs=[
                pl.BlockSpec(memory_space=pltpu.VMEM),
                pl.BlockSpec((slots, width, width), lambda s, *_: (s, 0, 0)),
            ],
            out_specs=pl.BlockSpec(memory_space=pltpu.VMEM),
        ),
        compiler_params=pltpu.CompilerParams(
            dimension_semantics=("arbitrary",), vmem_limit_bytes=36 * MIB
        ),
        cost_estimate=pl.CostEstimate(
            flops=n * width * width * exc * 16,
            bytes_accessed=n * width * width * 4 + panels.size * 4,
            transcendentals=0,
        ),
        name="block_products",
    )(slot_pairs.reshape(-1), lag_table, panels, kernel)


def scatter_kernel(side_a, side_b, per, t_ref, o_ref, buf1, buf2, buf3, sum2, sum3, s1, r1, s2, r2, s3, r3):
    r, a, b, core = place(side_b)
    width = t_ref.shape[2]
    greet(side_a, side_b, a, b, core)

    def row_of(a_, b_, c_):
        return (a_ * side_b + b_) * 2 + c_

    def part(row):
        return pl.ds(row * per, per)

    def remote(src, dst, ssem, rsem, target):
        return pltpu.make_async_remote_copy(
            src_ref=src, dst_ref=dst, send_sem=ssem, recv_sem=rsem,
            device_id={"row": target}, device_id_type=MESH,
        )

    sent = []
    order = [(d, e) for e in range(side_b - 1, -1, -1) for d in list(range(1, side_a)) + [0]]

    def at(d, e):
        return lax.rem(a + d, side_a), lax.rem(b + e, side_b)

    peer = row_of(a, b, 1 - core)

    def to_core(d, e):
        a_, b_ = at(d, e)
        chip = a_ * side_b + b_
        return remote(
            t_ref.at[part(row_of(a_, b_, 1 - core))], buf1.at[chip], s1.at[chip], r1.at[chip], peer
        )

    for d, e in order:
        c = to_core(d, e)
        c.start()
        sent.append(c)

    def core_sum(d, e):
        a_, b_ = at(d, e)
        to_core(d, e).wait_recv()
        return t_ref[part(row_of(a_, b_, core))] + buf1[a_ * side_b + b_]

    for d, e in order:
        a_, b_ = at(d, e)
        if e > 0:
            sum2[e - 1, d] = core_sum(d, e)
            c = remote(sum2.at[e - 1, d], buf2.at[b, a_], s2.at[e - 1, d], r2.at[b, a_], row_of(a, b_, core))
            c.start()
            sent.append(c)
            continue
        total = core_sum(d, 0)
        for e2 in range(1, side_b):
            from_b = lax.rem(b + e2, side_b)
            remote(
                sum2.at[e2 - 1, d], buf2.at[from_b, a_], s2.at[e2 - 1, d], r2.at[from_b, a_], row_of(a, from_b, core)
            ).wait_recv()
            total = total + buf2[from_b, a_]
        if d > 0:
            sum3[d] = total
            c = remote(sum3.at[d], buf3.at[a], s3.at[d], r3.at[a], row_of(a_, b, core))
            c.start()
            sent.append(c)
            continue
        sum3[0] = total
    for d in range(1, side_a):
        from_a = lax.rem(a + d, side_a)
        remote(sum3.at[d], buf3.at[from_a], s3.at[d], r3.at[from_a], row_of(from_a, b, core)).wait_recv()
    for m in range(per):
        total = sum3[0, m]
        for d in range(1, side_a):
            total = total + buf3[lax.rem(a + d, side_a), m]
        o_ref[:, m * width : (m + 1) * width] = total
    for c in sent:
        c.wait_send()


def scatter_sum(totals, rows, blocks):
    _, exc, width = totals.shape
    per = blocks // rows
    side_a, side_b = grid_of(rows)
    chips = side_a * side_b
    dma = pltpu.SemaphoreType.DMA
    return pl.pallas_call(
        functools.partial(scatter_kernel, side_a, side_b, per),
        out_shape=jax.ShapeDtypeStruct((exc, per * width), jnp.float32),
        in_specs=[pl.BlockSpec(memory_space=pltpu.VMEM)],
        out_specs=pl.BlockSpec(memory_space=pltpu.VMEM),
        scratch_shapes=[
            pltpu.VMEM((chips, per, exc, width), jnp.float32),
            pltpu.VMEM((side_b, side_a, per, exc, width), jnp.float32),
            pltpu.VMEM((side_a, per, exc, width), jnp.float32),
            pltpu.VMEM((max(side_b - 1, 1), side_a, per, exc, width), jnp.float32),
            pltpu.VMEM((side_a, per, exc, width), jnp.float32),
            dma((chips,)),
            dma((chips,)),
            dma((max(side_b - 1, 1), side_a)),
            dma((side_b, side_a)),
            dma((side_a,)),
            dma((side_a,)),
        ],
        compiler_params=pltpu.CompilerParams(
            collective_id=1, has_side_effects=True, vmem_limit_bytes=24 * MIB
        ),
        name="scatter_sum",
    )(totals)


def body(rows, slot_pairs, lag_table, kernel, history):
    width = kernel.shape[1]
    panels = gather_history(history, rows, width)
    totals = products(slot_pairs, lag_table, kernel, panels)
    return scatter_sum(totals, rows, panels.shape[1])


def solution(mesh):
    return jax.shard_map(
        functools.partial(body, mesh.shape["row"]),
        mesh=mesh,
        in_specs=(
            P(("grp", "row"), None),
            P("grp", None),
            P(("grp", "row"), None, None),
            P("grp", None, "row"),
        ),
        out_specs=P("grp", "row"),
        check_vma=False,
    )
```

```python
import functools

import jax
import jax.numpy as jnp
from jax import lax
from jax.experimental import pallas as pl
from jax.experimental.pallas import tpu as pltpu
from jax.sharding import PartitionSpec as P

MESH = pl.DeviceIdType.MESH
MIB = 1024 * 1024


def grid_of(rows):
    chips = rows // 2
    side_b = 1
    while side_b * side_b * 4 <= chips:
        side_b *= 2
    return chips // side_b, side_b


def place(side_b):
    r = lax.axis_index("row")
    core = lax.rem(r, 2)
    chip = r // 2
    return r, chip // side_b, lax.rem(chip, side_b), core


def greet(side_a, side_b, a, b, core):
    barrier = pltpu.get_barrier_semaphore()

    def signal(row):
        pl.semaphore_signal(barrier, inc=1, device_id={"row": row}, device_id_type=MESH)

    for d in range(1, side_a):
        signal((lax.rem(a + d, side_a) * side_b + b) * 2 + core)
    for d in range(1, side_b):
        signal((a * side_b + lax.rem(b + d, side_b)) * 2 + core)
    signal((a * side_b + b) * 2 + 1 - core)
    pl.semaphore_wait(barrier, side_a + side_b - 1)


def gather_kernel(side_a, side_b, group, h_ref, g_ref, own, own_sem, local_sem, z_sem, y_sem, c_sem, recv_sem):
    r, a, b, core = place(side_b)
    lags = h_ref.shape[0]
    width = g_ref.shape[3]
    per = h_ref.shape[2] // width
    parts = lags // group
    loads = [
        pltpu.make_async_copy(h_ref.at[:, :, pl.ds(m * width, width)], own.at[:, m], own_sem.at[m])
        for m in range(per)
    ]
    for c in loads:
        c.start()
    greet(side_a, side_b, a, b, core)
    for c in loads:
        c.wait()

    def row_of(a_, b_, c_):
        return (a_ * side_b + b_) * 2 + c_

    def chunk(k, row):
        return g_ref.at[pl.ds(k * group, group), pl.ds(row * per, per)]

    def copy(k, origin, target, send, mine=False):
        src = own.at[pl.ds(k * group, group)] if mine else chunk(k, origin)
        return pltpu.make_async_remote_copy(
            src_ref=src,
            dst_ref=chunk(k, origin),
            send_sem=send,
            recv_sem=recv_sem.at[k, origin],
            device_id={"row": target},
            device_id_type=MESH,
        )

    def arrived(k, origin):
        copy(k, origin, row_of(a, b, 1 - core), c_sem.at[k, 0]).wait_recv()

    def inside(a_):
        return jnp.logical_and(a_ >= 0, a_ < side_a)

    hops = [(1, 0)] + [(sign, d) for d in range(1, side_a) for sign in (1, -1)]

    def along(k, sign, d, act):
        @pl.when(inside(a + sign))
        def _():
            act(copy(k, row_of(a - sign * d, b, core), row_of(a + sign, b, core), z_sem.at[k, (sign + 1) // 2, d], d == 0))

    def beside(k, sign, d, act):
        origin = row_of(a - sign * d, b, core)
        for e in range(1, side_b):
            act(copy(k, origin, row_of(a, lax.rem(b + e, side_b), core), y_sem.at[k, a - sign * d, e], d == 0))

    def to_core(k, origin, act, mine=False):
        act(copy(k, origin, row_of(a, b, 1 - core), c_sem.at[k, origin // 2], mine))

    def start(c):
        c.start()

    def finish(c):
        c.wait_send()

    local = []
    for k in range(parts):
        along(k, 1, 0, start)
        along(k, -1, 0, start)
        beside(k, 1, 0, start)
        to_core(k, r, start, True)
        c = pltpu.make_async_copy(own.at[pl.ds(k * group, group)], chunk(k, r), local_sem.at[k])
        c.start()
        local.append(c)

    def column(k):
        for sign, d in hops[1:]:

            @pl.when(inside(a - sign * d))
            def _():
                origin = row_of(a - sign * d, b, core)
                arrived(k, origin)
                along(k, sign, d, start)
                beside(k, sign, d, start)
                to_core(k, origin, start)

    def across(k):
        for sign, d in hops:

            @pl.when(inside(a - sign * d))
            def _():
                for e in range(1, side_b):
                    origin = row_of(a - sign * d, lax.rem(b + e, side_b), core)
                    arrived(k, origin)
                    to_core(k, origin, start)

    for k in range(parts):
        column(k)
        if k > 0:
            across(k - 1)
    across(parts - 1)
    for k in range(parts):
        along(k, 1, 0, finish)
        along(k, -1, 0, finish)
        beside(k, 1, 0, finish)
        for sign, d in hops[1:]:

            @pl.when(inside(a - sign * d))
            def _():
                along(k, sign, d, finish)
                beside(k, sign, d, finish)

        for a_ in range(side_a):
            for b_ in range(side_b):
                arrived(k, row_of(a_, b_, 1 - core))
                to_core(k, row_of(a_, b_, core), finish)
    for c in local:
        c.wait()


def gather_history(history, rows, width):
    lags, exc, local = history.shape
    per = local // width
    side_a, side_b = grid_of(rows)
    group = 1 if rows <= 16 else lags
    parts = lags // group
    return pl.pallas_call(
        functools.partial(gather_kernel, side_a, side_b, group),
        out_shape=jax.ShapeDtypeStruct((lags, rows * per, exc, width), jnp.float32),
        in_specs=[pl.BlockSpec(memory_space=pltpu.HBM)],
        out_specs=pl.BlockSpec(memory_space=pltpu.VMEM),
        scratch_shapes=[
            pltpu.VMEM((lags, per, exc, width), jnp.float32),
            pltpu.SemaphoreType.DMA((per,)),
            pltpu.SemaphoreType.DMA((parts,)),
            pltpu.SemaphoreType.DMA((parts, 2, side_a)),
            pltpu.SemaphoreType.DMA((parts, side_a, side_b)),
            pltpu.SemaphoreType.DMA((parts, side_a * side_b)),
            pltpu.SemaphoreType.DMA((parts, rows)),
        ],
        compiler_params=pltpu.CompilerParams(collective_id=0, has_side_effects=True, vmem_limit_bytes=24 * MIB),
        name="gather_history",
    )(history)


def split(x):
    hi = x.astype(jnp.bfloat16)
    lo = (x - hi.astype(jnp.float32)).astype(jnp.bfloat16)
    return hi, lo


def product_kernel(slots, pairs, lag, g_ref, k_ref, t_ref):
    step = pl.program_id(0)
    exc = g_ref.shape[2]
    blocks = g_ref.shape[1]

    @pl.when(step == 0)
    def _():
        t_ref[...] = jnp.zeros_like(t_ref)

    def panel(k, col):
        hi, lo = split(g_ref[k, col])
        return jnp.concatenate(
            [jnp.concatenate([hi, hi], axis=1), jnp.concatenate([lo, lo], axis=1)], axis=0
        )

    for q in range(slots):
        s = step * slots + q
        i = pairs[0, s]
        j = pairs[1, s]
        live = i >= 0
        row = jnp.maximum(i, 0)
        col = jnp.maximum(j, 0)
        k = lag[row, col]
        hi, lo = split(k_ref[q])
        far = lax.dot_general(
            panel(k, col),
            jnp.concatenate([hi, lo], axis=1),
            (((1,), (1,)), ((), ())),
            preferred_element_type=jnp.float32,
        )
        near = lax.dot_general(
            panel(k, row),
            jnp.concatenate([hi, lo], axis=0),
            (((1,), (0,)), ((), ())),
            preferred_element_type=jnp.float32,
        )
        to_row = jnp.where(live, i, blocks)
        to_col = jnp.where(jnp.logical_and(live, i != j), j, blocks)
        t_ref[to_row] += far[:exc] + far[exc:]
        t_ref[to_col] += near[:exc] + near[exc:]


def products(slot_pairs, lag_table, kernel, panels):
    n = kernel.shape[0]
    width = kernel.shape[1]
    lags, blocks, exc, _ = panels.shape
    slots = max(d for d in range(1, 87) if n % d == 0)
    return pl.pallas_call(
        functools.partial(product_kernel, slots),
        out_shape=jax.ShapeDtypeStruct((blocks + 1, exc, width), jnp.float32),
        grid_spec=pltpu.PrefetchScalarGridSpec(
            num_scalar_prefetch=2,
            grid=(n // slots,),
            in_specs=[
                pl.BlockSpec(memory_space=pltpu.VMEM),
                pl.BlockSpec((slots, width, width), lambda s, *_: (s, 0, 0)),
            ],
            out_specs=pl.BlockSpec(memory_space=pltpu.VMEM),
        ),
        compiler_params=pltpu.CompilerParams(
            dimension_semantics=("arbitrary",), vmem_limit_bytes=36 * MIB
        ),
        cost_estimate=pl.CostEstimate(
            flops=n * width * width * exc * 16,
            bytes_accessed=n * width * width * 4 + panels.size * 4,
            transcendentals=0,
        ),
        name="block_products",
    )(slot_pairs.T, lag_table, panels, kernel)


def scatter_kernel(side_a, side_b, per, t_ref, o_ref, buf1, buf2, buf3, sum2, sum3, s1, r1, s2, r2, s3, r3):
    r, a, b, core = place(side_b)
    width = t_ref.shape[2]
    greet(side_a, side_b, a, b, core)

    def row_of(a_, b_, c_):
        return (a_ * side_b + b_) * 2 + c_

    def part(row):
        return pl.ds(row * per, per)

    def remote(src, dst, ssem, rsem, target):
        return pltpu.make_async_remote_copy(
            src_ref=src, dst_ref=dst, send_sem=ssem, recv_sem=rsem,
            device_id={"row": target}, device_id_type=MESH,
        )

    sent = []
    order = [(d, e) for e in range(side_b - 1, -1, -1) for d in list(range(1, side_a)) + [0]]

    def at(d, e):
        return lax.rem(a + d, side_a), lax.rem(b + e, side_b)

    peer = row_of(a, b, 1 - core)

    def to_core(d, e):
        a_, b_ = at(d, e)
        chip = a_ * side_b + b_
        return remote(
            t_ref.at[part(row_of(a_, b_, 1 - core))], buf1.at[chip], s1.at[chip], r1.at[chip], peer
        )

    for d, e in order:
        c = to_core(d, e)
        c.start()
        sent.append(c)

    def core_sum(d, e):
        a_, b_ = at(d, e)
        to_core(d, e).wait_recv()
        return t_ref[part(row_of(a_, b_, core))] + buf1[a_ * side_b + b_]

    for d, e in order:
        a_, b_ = at(d, e)
        if e > 0:
            sum2[e - 1, d] = core_sum(d, e)
            c = remote(sum2.at[e - 1, d], buf2.at[b, a_], s2.at[e - 1, d], r2.at[b, a_], row_of(a, b_, core))
            c.start()
            sent.append(c)
            continue
        total = core_sum(d, 0)
        for e2 in range(1, side_b):
            from_b = lax.rem(b + e2, side_b)
            remote(
                sum2.at[e2 - 1, d], buf2.at[from_b, a_], s2.at[e2 - 1, d], r2.at[from_b, a_], row_of(a, from_b, core)
            ).wait_recv()
            total = total + buf2[from_b, a_]
        if d > 0:
            sum3[d] = total
            c = remote(sum3.at[d], buf3.at[a], s3.at[d], r3.at[a], row_of(a_, b, core))
            c.start()
            sent.append(c)
            continue
        sum3[0] = total
    for d in range(1, side_a):
        from_a = lax.rem(a + d, side_a)
        remote(sum3.at[d], buf3.at[from_a], s3.at[d], r3.at[from_a], row_of(from_a, b, core)).wait_recv()
    for m in range(per):
        total = sum3[0, m]
        for d in range(1, side_a):
            total = total + buf3[lax.rem(a + d, side_a), m]
        o_ref[:, m * width : (m + 1) * width] = total
    for c in sent:
        c.wait_send()


def scatter_sum(totals, rows, blocks):
    _, exc, width = totals.shape
    per = blocks // rows
    side_a, side_b = grid_of(rows)
    chips = side_a * side_b
    dma = pltpu.SemaphoreType.DMA
    return pl.pallas_call(
        functools.partial(scatter_kernel, side_a, side_b, per),
        out_shape=jax.ShapeDtypeStruct((exc, per * width), jnp.float32),
        in_specs=[pl.BlockSpec(memory_space=pltpu.VMEM)],
        out_specs=pl.BlockSpec(memory_space=pltpu.VMEM),
        scratch_shapes=[
            pltpu.VMEM((chips, per, exc, width), jnp.float32),
            pltpu.VMEM((side_b, side_a, per, exc, width), jnp.float32),
            pltpu.VMEM((side_a, per, exc, width), jnp.float32),
            pltpu.VMEM((max(side_b - 1, 1), side_a, per, exc, width), jnp.float32),
            pltpu.VMEM((side_a, per, exc, width), jnp.float32),
            dma((chips,)),
            dma((chips,)),
            dma((max(side_b - 1, 1), side_a)),
            dma((side_b, side_a)),
            dma((side_a,)),
            dma((side_a,)),
        ],
        compiler_params=pltpu.CompilerParams(
            collective_id=1, has_side_effects=True, vmem_limit_bytes=24 * MIB
        ),
        name="scatter_sum",
    )(totals)


def body(rows, slot_pairs, lag_table, kernel, history):
    width = kernel.shape[1]
    panels = gather_history(history, rows, width)
    totals = products(slot_pairs, lag_table, kernel, panels)
    return scatter_sum(totals, rows, panels.shape[1])


def solution(mesh):
    return jax.shard_map(
        functools.partial(body, mesh.shape["row"]),
        mesh=mesh,
        in_specs=(
            P(("grp", "row"), None),
            P("grp", None),
            P(("grp", "row"), None, None),
            P("grp", None, "row"),
        ),
        out_specs=P("grp", "row"),
        check_vma=False,
    )
```
